32 devices in a mesh: seq: 8 (over y, x, core), head: 4 (over z).
Axes of the slice: x: 2, y: 2, z: 4, core: 2. Of those that a mesh axis runs over, the one named last changes fastest.
Arguments:
- tokens: bfloat16 [2, 8192, 2048], P(None, ('seq', 'head')), may hold values from -6 to 6
- norm_gain: float32 [2048], replicated, may hold values from 0.25 to 1.75
- projection: bfloat16 [2048, 6144], P(None, 'head'), may hold values from -0.125 to 0.125
- level_table: float32 [16, 16, 18], P(None, 'head'), may hold values from 0.05 to 1
- level_index: int32 [2, 8192], P(None, 'seq'), may hold values from 0 to 15
- lengths: int32 [2], replicated, may hold values from 4096 to 8192, as said below
Outputs:
- attended: bfloat16 [2, 8192, 2048], P(None, 'seq', 'head')
The draws below stay inside these ranges and needn't reach their ends.
Inputs may be any that keep to these rules, and one draw needn't show every extreme that they name: The first sequence is always whole: lengths[0] = 8192.
All inputs are finite; a program needn't handle non-finite values.
Results may differ from the reference program's by a relative error of at most 0.0097.
Values may be sent and summed in bfloat16 or wider, within the bound.
A program may use at most 128 MiB of HBM per device.

```python
import math
import jax
import jax.numpy as jnp
from jax import lax

D = 2048
H = 16
DH = 128
SEQS = 2
SPAN = 512
TABLES = 16
LEVELS = 18
LEN = 8192


def draw_lengths(key, part):
    others = jax.random.randint(jax.random.fold_in(key, 7), (SEQS - 1,), LEN // 2, LEN + 1, dtype=jnp.int32)
    return jnp.concatenate([jnp.full((1,), LEN, jnp.int32), others])


def plant(values, key, least, largest):
    spot = [jax.random.randint(jax.random.fold_in(key, axis), (), 0, length) for axis, length in enumerate(values.shape)]
    main_axis = values.shape.index(max(values.shape))
    next_to = spot[:main_axis] + [(spot[main_axis] + 1) % values.shape[main_axis]] + spot[main_axis + 1:]
    return values.at[tuple(spot)].set(least).at[tuple(next_to)].set(largest)


def block_levels(stream_key, dims, pieces, least, largest):
    loudness = 1.0
    for axis_at, blocks in pieces:
        draws = jax.random.uniform(jax.random.fold_in(jax.random.fold_in(stream_key, 6), axis_at), (blocks,), jnp.float32, least / len(pieces), largest / len(pieces))
        loudness = loudness * jnp.repeat(jnp.exp(draws), dims[axis_at] // blocks).reshape((-1,) + (1,) * (len(dims) - 1 - axis_at))
    return loudness


def normal_values(own_key, extent, scale, most, cuts=(), held_as=jnp.bfloat16):
    drawn = jax.random.normal(own_key, extent, jnp.float32) * scale
    if len(cuts) > 0:
        drawn = block_levels(own_key, extent, cuts, -0.22, 0.18) * drawn
    return jnp.clip(drawn, min=-most, max=most).astype(held_as)


def setup_inputs(seed: int = 0) -> dict:
    splits = jax.random.split(jax.random.key(seed), 7)
    tokens = normal_values(splits[0], (SEQS, LEN, D), 1.0, 6.0, ((1, 32),))
    norm_gain = jnp.clip(1.0 + 0.15 * jax.random.normal(splits[1], (D,), jnp.float32), 0.25, 1.75)
    projection = normal_values(splits[2], (D, 3 * D), D ** -0.5, 0.125, ((1, 4),))
    level_table = jnp.clip(jnp.exp(math.log(1.0) - 2.9957323 * jax.random.uniform(splits[3], (TABLES, H, LEVELS), jnp.float32) ** block_levels(splits[3], (TABLES, H, LEVELS), ((1, 4),), -0.2, 0.2)), 0.05, 1.0)
    level_index = plant(jax.random.randint(splits[4], (SEQS, LEN), 0, TABLES), jax.random.fold_in(splits[4], 1), 0, TABLES - 1).astype(jnp.int32)
    lengths = draw_lengths(jax.random.fold_in(splits[6], 71), 0)
    return dict(tokens=tokens, norm_gain=norm_gain, projection=projection, level_table=level_table, level_index=level_index, lengths=lengths)


def digit_count(values, limit):
    counted = jnp.zeros(values.shape, jnp.int32)
    for shift in range(limit):
        counted = counted + (values >= 1 << shift).astype(jnp.int32)
    return counted

def reference(tokens, norm_gain, projection, level_table, level_index, lengths):
    widened = tokens.astype(jnp.float32)
    normed = (widened * lax.rsqrt(lax.optimization_barrier(jnp.mean(widened * widened, -1, keepdims=True)) + 1e-06) * norm_gain).astype(jnp.bfloat16)

    def project_one(rows_seq):
        return jnp.dot(rows_seq, projection, preferred_element_type=jnp.float32).astype(jnp.bfloat16)
    projected = lax.map(project_one, normed).reshape(SEQS, LEN, H, 3, DH)
    projected = projected.transpose(2, 3, 0, 1, 4)
    weights = level_table[level_index].transpose(2, 0, 1, 3)
    span_total = LEN // SPAN
    span_bits = span_total.bit_length() - 1
    lchunk = SPAN.bit_length() - 1
    positions = jnp.arange(SPAN, dtype=jnp.int32)
    level_grid = digit_count(jnp.bitwise_xor(positions[:, None], positions[None, :]), lchunk + 1)
    causal = (positions[:, None] >= positions[None, :]).astype(jnp.float32)
    span_ids = jnp.arange(span_total, dtype=jnp.int32)
    span_dist = digit_count(jnp.bitwise_xor(span_ids[:, None], span_ids[None, :]), span_bits + 1)
    span_earlier = span_ids[None, :] < span_ids[:, None]
    span_mask = jnp.stack([((span_dist == step + 1) & span_earlier).astype(jnp.float32) for step in range(span_bits)])
    highest = lax.Precision.HIGHEST

    def one_head(inputs):
        head_qkv, head_weights = inputs
        queries = head_qkv[0].reshape(SEQS, span_total, SPAN, DH).astype(jnp.float32)
        keys_here = head_qkv[1].reshape(SEQS, span_total, SPAN, DH).astype(jnp.float32)
        values_here = head_qkv[2].reshape(SEQS, span_total, SPAN, DH).astype(jnp.float32)
        level_weight = head_weights.reshape(SEQS, span_total, SPAN, LEVELS)
        scores = jnp.einsum('sctd,scud->sctu', queries, keys_here, precision=highest)
        grid = jnp.zeros(scores.shape, jnp.float32)
        for level_step in range(lchunk + 1):
            grid = grid + level_weight[..., level_step][..., None] * (level_grid == level_step).astype(jnp.float32)
        weighted = (scores * grid * causal).astype(jnp.bfloat16).astype(jnp.float32)
        near_part = jnp.einsum('sctu,scue->scte', weighted, values_here, precision=highest)
        states = jnp.einsum('sctd,scte->scde', keys_here, values_here, precision=highest)
        far_part = jnp.zeros(near_part.shape, jnp.float32)
        for level_step in range(span_bits):
            bucket = jnp.einsum('cb,sbde->scde', span_mask[level_step], states, precision=highest)
            bucket = bucket.astype(jnp.bfloat16).astype(jnp.float32)
            readout = jnp.einsum('sctd,scde->scte', queries, bucket, precision=highest)
            far_part = far_part + level_weight[..., lchunk + 1 + level_step][..., None] * readout
        output = near_part + far_part
        output = output * lax.rsqrt(lax.optimization_barrier(jnp.mean(output * output, -1, keepdims=True)) + 1e-06)
        return output.reshape(SEQS, LEN, DH)
    heads_out = lax.map(one_head, (projected, weights))
    attended = heads_out.transpose(1, 2, 0, 3).reshape(SEQS, LEN, D)
    valid = jnp.arange(LEN, dtype=jnp.int32)[None, :] < lengths[:, None]
    return jnp.where(valid[..., None], attended, 0.0).astype(jnp.bfloat16)
```

```python
import functools

import jax
import jax.numpy as jnp
from jax import lax
from jax.experimental import pallas as pl
from jax.experimental.pallas import tpu as pltpu
from jax.sharding import PartitionSpec as P

SPAN = 512
LANE = 128
STRIDE = 32
VMEM_LIMIT = 56 * 1024 * 1024
NT = (((1,), (1,)), ((), ()))
TN = (((0,), (0,)), ((), ()))


def swapped(array, axis, bit):
    return lax.ppermute(array, axis, [(i, i ^ 1 << bit) for i in range(lax.axis_size(axis))])


def dot32(a, b):
    return jnp.dot(a, b, preferred_element_type=jnp.float32)


def near_kernel(
    heads, head_size, rows_ref, gain_ref, proj_ref, weight_ref, q_ref, near_ref, total_ref, normed, qkv
):
    span = pl.program_id(0)
    lchunk = SPAN.bit_length() - 1

    @pl.when(span == 0)
    def _():
        total_ref[...] = jnp.zeros_like(total_ref)

    piece = 128
    for start in range(0, SPAN, piece):
        x = rows_ref[start : start + piece].astype(jnp.float32)
        scale = lax.rsqrt(jnp.mean(x * x, -1, keepdims=True) + 1e-06)
        normed[start : start + piece] = (x * scale * gain_ref[...]).astype(jnp.bfloat16)
    width = proj_ref.shape[1]
    step = 2 * 3 * head_size if width % (6 * head_size) == 0 else 3 * head_size
    for col in range(0, width, step):
        qkv[:, col : col + step] = dot32(normed[...], proj_ref[:, col : col + step]).astype(
            jnp.bfloat16
        )

    t = lax.broadcasted_iota(jnp.int32, (LANE, LANE), 0)
    u = lax.broadcasted_iota(jnp.int32, (LANE, LANE), 1)
    apart = t ^ u
    level = jnp.zeros((LANE, LANE), jnp.int32)
    for shift in range(LANE.bit_length() - 1):
        level = level + (apart >= 1 << shift).astype(jnp.int32)
    level = jnp.where(u <= t, level, STRIDE - 1)

    for h in range(heads):
        base = h * 3 * head_size
        q = qkv[:, base : base + head_size]
        k = qkv[:, base + head_size : base + 2 * head_size]
        v = qkv[:, base + 2 * head_size : base + 3 * head_size]
        out_cols = slice(h * head_size, (h + 1) * head_size)
        q_ref[:, out_cols] = q
        before = total_ref[h]
        readout = dot32(q, before.astype(jnp.bfloat16))
        for start in range(0, SPAN, LANE):
            rows = slice(start, start + LANE)
            w_rows = weight_ref[rows, :]
            grid = jnp.take_along_axis(w_rows, level + h * STRIDE, axis=1)
            scores = lax.dot_general(q[rows], k[rows], NT, preferred_element_type=jnp.float32)
            acc = dot32((scores * grid).astype(jnp.bfloat16), v[rows])
            far_at = h * STRIDE + lchunk + 1
            acc = acc + w_rows[:, far_at : far_at + 1] * readout[rows]
            size = LANE
            while size < SPAN:
                if start & size:
                    low = start & ~(2 * size - 1)
                    at = h * STRIDE + size.bit_length()
                    scores = lax.dot_general(
                        q[rows], k[low : low + size], NT, preferred_element_type=jnp.float32
                    )
                    scores = (scores * w_rows[:, at : at + 1]).astype(jnp.bfloat16)
                    acc = acc + dot32(scores, v[low : low + size])
                size *= 2
            near_ref[rows, out_cols] = acc
        total_ref[h] = before + lax.dot_general(k, v, TN, preferred_element_type=jnp.float32)


def near_call(rows, gain, projection, weights, heads, head_size):
    length, model_width = rows.shape
    width = projection.shape[1]
    out_width = heads * head_size
    return pl.pallas_call(
        functools.partial(near_kernel, heads, head_size),
        grid=(length // SPAN,),
        in_specs=[
            pl.BlockSpec((SPAN, model_width), lambda c: (c, 0)),
            pl.BlockSpec((1, model_width), lambda c: (0, 0)),
            pl.BlockSpec((model_width, width), lambda c: (0, 0)),
            pl.BlockSpec((SPAN, weights.shape[1]), lambda c: (c, 0)),
        ],
        out_specs=[
            pl.BlockSpec((SPAN, out_width), lambda c: (c, 0)),
            pl.BlockSpec((SPAN, out_width), lambda c: (c, 0)),
            pl.BlockSpec((heads, head_size, head_size), lambda c: (0, 0, 0)),
        ],
        out_shape=[
            jax.ShapeDtypeStruct((length, out_width), jnp.bfloat16),
            jax.ShapeDtypeStruct((length, out_width), jnp.float32),
            jax.ShapeDtypeStruct((heads, head_size, head_size), jnp.float32),
        ],
        scratch_shapes=[
            pltpu.VMEM((SPAN, model_width), jnp.bfloat16),
            pltpu.VMEM((SPAN, width), jnp.bfloat16),
        ],
        compiler_params=pltpu.CompilerParams(vmem_limit_bytes=VMEM_LIMIT),
        cost_estimate=pl.CostEstimate(
            flops=2 * length * model_width * width + 2 * length * out_width * SPAN,
            bytes_accessed=2 * length * model_width + 2 * model_width * width + 6 * length * out_width,
            transcendentals=0,
        ),
        name="near",
    )(rows, gain, projection, weights)


def far_kernel(heads, head_size, level_count, first_level, seq, held, *refs):
    scalar_ref, q_ref, near_ref, weight_ref = refs[:4]
    sibling_refs = refs[4 : 4 + level_count]
    out_ref = refs[-1]
    own = scalar_ref[0]
    rows = q_ref.shape[0]
    start = own * (rows * pl.num_programs(0)) + pl.program_id(0) * rows
    valid = start + lax.broadcasted_iota(jnp.int32, (rows, 1), 0) < scalar_ref[1 + seq]
    for h in range(heads):
        cols = slice(h * head_size, (h + 1) * head_size)
        q = q_ref[:, cols]
        acc = near_ref[:, cols]
        for j in range(level_count):
            upper = ((own >> j) & 1) == 1
            bucket = jnp.where(upper, sibling_refs[j][h], 0.0).astype(jnp.bfloat16)
            at = h * STRIDE + first_level + j
            acc = acc + weight_ref[:, at : at + 1] * dot32(q, bucket)
        acc = acc * lax.rsqrt(jnp.mean(acc * acc, -1, keepdims=True) + 1e-06)
        out_ref[0, :, cols] = jnp.where(valid, acc, 0.0).astype(jnp.bfloat16)


def far_call(seq, batch, held, scalars, q, near, weights, siblings, first_level, heads, head_size):
    length, out_width = q.shape
    tile = min(SPAN, length)
    spec = pl.BlockSpec((tile, out_width), lambda c: (c, 0))
    in_specs = [
        pl.BlockSpec(memory_space=pltpu.SMEM),
        spec,
        spec,
        pl.BlockSpec((tile, weights.shape[1]), lambda c: (c, 0)),
    ] + [pl.BlockSpec((heads, head_size, head_size), lambda c: (0, 0, 0)) for _ in siblings]
    operands = [scalars, q, near, weights, *siblings]
    aliases = {}
    if held is not None:
        aliases = {len(operands): 0}
        operands.append(held)
        in_specs.append(pl.BlockSpec(memory_space=pl.ANY))
    return pl.pallas_call(
        functools.partial(
            far_kernel, heads, head_size, len(siblings), first_level, seq, held is not None
        ),
        grid=(length // tile,),
        in_specs=in_specs,
        out_specs=pl.BlockSpec((1, tile, out_width), lambda c: (seq, c, 0)),
        out_shape=jax.ShapeDtypeStruct((batch, length, out_width), jnp.bfloat16),
        input_output_aliases=aliases,
        compiler_params=pltpu.CompilerParams(vmem_limit_bytes=VMEM_LIMIT),
        cost_estimate=pl.CostEstimate(
            flops=2 * length * out_width * head_size * len(siblings),
            bytes_accessed=8 * length * out_width,
            transcendentals=0,
        ),
        name="far",
    )(*operands)


def on_device(tokens, norm_gain, projection, level_table, level_index, lengths):
    batch_seqs, row_count, model_width = tokens.shape
    table_count, heads, level_total = level_table.shape
    head_size = projection.shape[1] // (3 * heads)
    block_len = row_count * lax.axis_size("head")
    span_count = block_len // SPAN
    local_bits = span_count.bit_length() - 1
    lchunk = SPAN.bit_length() - 1
    seq_bits = lax.axis_size("seq").bit_length() - 1
    own_index = lax.axis_index("seq")

    gathered = [
        lax.all_gather(tokens[s], "head", axis=0, tiled=True) for s in range(batch_seqs)
    ]
    table = jnp.pad(level_table, ((0, 0), (0, 0), (0, STRIDE - level_total)))
    table = table.reshape(table_count, heads * STRIDE)
    onehot = (level_index[..., None] == jnp.arange(table_count, dtype=jnp.int32)).astype(
        jnp.float32
    )
    weights = [
        jnp.dot(onehot[s], table, precision=lax.Precision.HIGHEST) for s in range(batch_seqs)
    ]
    scalars = jnp.concatenate([own_index.astype(jnp.int32)[None], lengths])
    gain = norm_gain[None]

    attended = None
    for s in range(batch_seqs):
        q, near, total = near_call(gathered[s], gain, projection, weights[s], heads, head_size)
        siblings = []
        block_sum = total
        for bit in range(seq_bits):
            sibling = swapped(block_sum, "seq", bit)
            siblings.append(sibling)
            block_sum = block_sum + sibling
        attended = far_call(
            s, batch_seqs, attended, scalars, q, near, weights[s], siblings,
            lchunk + local_bits + 1, heads, head_size,
        )
    return attended


def solution(mesh):
    in_specs = (
        P(None, ("seq", "head"), None),
        P(),
        P(None, "head"),
        P(None, "head", None),
        P(None, "seq"),
        P(),
    )
    out_specs = P(None, "seq", "head")
    return jax.shard_map(
        on_device, mesh=mesh, in_specs=in_specs, out_specs=out_specs, check_vma=False
    )
```

```python
import functools

import jax
import jax.numpy as jnp
from jax import lax
from jax.experimental import pallas as pl
from jax.experimental.pallas import tpu as pltpu
from jax.sharding import PartitionSpec as P

SPAN = 512
LANE = 128
STRIDE = 32
VMEM_LIMIT = 56 * 1024 * 1024
NT = (((1,), (1,)), ((), ()))
TN = (((0,), (0,)), ((), ()))
MESH = pl.DeviceIdType.MESH


def dot32(a, b):
    return jnp.dot(a, b, preferred_element_type=jnp.float32)


def kernel(
    dims,
    tokens_ref, gain_ref, proj_hbm, table_ref, index_ref, lengths_ref,
    out_ref,
    rows_buf, proj_ref, normed, qkv, near, weights, total, outbox, inbox,
    own_sem, proj_sem, send_sem, recv_sem, tree_send, tree_recv,
):
    heads, head_size, groups, seq_bits, span_count = dims
    batch, row_count, model_width = tokens_ref.shape
    block_len = row_count * groups
    width = proj_ref.shape[1]
    lchunk = SPAN.bit_length() - 1
    local_bits = span_count.bit_length() - 1
    first_level = lchunk + local_bits + 1
    me = lax.axis_index("head")
    own = lax.axis_index("seq")

    def flipped(bit):
        return own + (1 << bit) - 2 * (own & (1 << bit))

    proj_copy = pltpu.make_async_copy(proj_hbm, proj_ref, proj_sem)
    barrier = pltpu.get_barrier_semaphore()

    @pl.when(me > 0)
    def _():
        pl.semaphore_signal(barrier, inc=1, device_id={"head": me - 1}, device_id_type=MESH)

    @pl.when(me < groups - 1)
    def _():
        pl.semaphore_signal(barrier, inc=1, device_id={"head": me + 1}, device_id_type=MESH)

    for bit in range(seq_bits):
        pl.semaphore_signal(barrier, inc=1, device_id={"seq": flipped(bit)}, device_id_type=MESH)

    def own_copy(s):
        return pltpu.make_async_copy(tokens_ref.at[s], rows_buf.at[s, me], own_sem.at[s])

    for s in range(batch):
        own_copy(s).start()
    proj_copy.start()
    ends = (me == 0).astype(jnp.int32) + (me == groups - 1).astype(jnp.int32)
    pl.semaphore_wait(barrier, seq_bits + 2 - ends)

    def send_own(side, s):
        return pltpu.make_async_remote_copy(
            src_ref=tokens_ref.at[s], dst_ref=rows_buf.at[s, me],
            send_sem=send_sem.at[side, s, me], recv_sem=recv_sem.at[s, me],
            device_id={"head": me + 1 - 2 * side}, device_id_type=MESH,
        )

    def pass_on(side, s, owner):
        return pltpu.make_async_remote_copy(
            src_ref=rows_buf.at[s, owner], dst_ref=rows_buf.at[s, owner],
            send_sem=send_sem.at[side, s, owner], recv_sem=recv_sem.at[s, owner],
            device_id={"head": me + 1 - 2 * side}, device_id_type=MESH,
        )

    def has_next(side):
        return me < groups - 1 if side == 0 else me > 0

    for s in range(batch):
        for side in range(2):
            @pl.when(has_next(side))
            def _():
                send_own(side, s).start()

    proj_copy.wait()

    def project(s, owner):
        piece = 128
        for start in range(0, row_count, piece):
            x = rows_buf[s, owner, start : start + piece].astype(jnp.float32)
            scale = lax.rsqrt(jnp.mean(x * x, -1, keepdims=True) + 1e-06)
            normed[start : start + piece] = (x * scale * gain_ref[...]).astype(jnp.bfloat16)
        step = 2 * 3 * head_size if width % (6 * head_size) == 0 else 3 * head_size
        at = pl.ds(pl.multiple_of(owner * row_count, row_count), row_count)
        for col in range(0, width, step):
            qkv[s, at, col : col + step] = dot32(
                normed[...], proj_ref[:, col : col + step]
            ).astype(jnp.bfloat16)

    t = lax.broadcasted_iota(jnp.int32, (LANE, LANE), 0)
    u = lax.broadcasted_iota(jnp.int32, (LANE, LANE), 1)
    apart = t ^ u
    level = jnp.zeros((LANE, LANE), jnp.int32)
    for shift in range(LANE.bit_length() - 1):
        level = level + (apart >= 1 << shift).astype(jnp.int32)
    level = jnp.where(u <= t, level, STRIDE - 1)

    def near_span(s, span):
        base_row = span * SPAN
        at_span = pl.ds(pl.multiple_of(base_row, SPAN), SPAN)
        choice = index_ref[s, at_span, :]
        tables = lax.broadcasted_iota(jnp.int32, (SPAN, table_ref.shape[0]), 1)
        onehot = (choice == tables).astype(jnp.float32)
        weights[at_span, :] = jnp.dot(
            onehot, table_ref[...], precision=lax.Precision.HIGHEST,
            preferred_element_type=jnp.float32,
        )
        for h in range(heads):
            base = h * 3 * head_size
            q = qkv[s, at_span, base : base + head_size]
            k = qkv[s, at_span, base + head_size : base + 2 * head_size]
            v = qkv[s, at_span, base + 2 * head_size : base + 3 * head_size]
            out_cols = slice(h * head_size, (h + 1) * head_size)
            before = total[h]
            readout = dot32(q, before.astype(jnp.bfloat16))
            for start in range(0, SPAN, LANE):
                rows = slice(start, start + LANE)
                at_rows = pl.ds(pl.multiple_of(base_row + start, LANE), LANE)
                w_rows = weights[at_rows, :]
                grid = jnp.take_along_axis(w_rows, level + h * STRIDE, axis=1)
                scores = lax.dot_general(q[rows], k[rows], NT, preferred_element_type=jnp.float32)
                acc = dot32((scores * grid).astype(jnp.bfloat16), v[rows])
                far_at = h * STRIDE + lchunk + 1
                acc = acc + w_rows[:, far_at : far_at + 1] * readout[rows]
                size = LANE
                while size < SPAN:
                    if start & size:
                        low = start & ~(2 * size - 1)
                        at = h * STRIDE + size.bit_length()
                        scores = lax.dot_general(
                            q[rows], k[low : low + size], NT, preferred_element_type=jnp.float32
                        )
                        scores = (scores * w_rows[:, at : at + 1]).astype(jnp.bfloat16)
                        acc = acc + dot32(scores, v[low : low + size])
                    size *= 2
                near[at_rows, out_cols] = acc
            total[h] = before + lax.dot_general(k, v, TN, preferred_element_type=jnp.float32)

    def exchange(s, bit):
        return pltpu.make_async_remote_copy(
            src_ref=outbox.at[s, bit], dst_ref=inbox.at[s, bit],
            send_sem=tree_send.at[s, bit], recv_sem=tree_recv.at[s, bit],
            device_id={"seq": flipped(bit)}, device_id_type=MESH,
        )

    def far_span(s, span):
        base_row = span * SPAN
        at_span = pl.ds(pl.multiple_of(base_row, SPAN), SPAN)
        first = own * block_len + base_row
        valid = first + lax.broadcasted_iota(jnp.int32, (SPAN, 1), 0) < lengths_ref[s]
        w_rows = weights[at_span, :]
        for h in range(heads):
            cols = slice(h * head_size, (h + 1) * head_size)
            base = h * 3 * head_size
            q = qkv[s, at_span, base : base + head_size]
            acc = near[at_span, cols]
            for j in range(seq_bits):
                upper = ((own >> j) & 1) == 1
                bucket = jnp.where(upper, inbox[s, j, h].astype(jnp.float32), 0.0)
                at = h * STRIDE + first_level + j
                acc = acc + w_rows[:, at : at + 1] * dot32(q, bucket.astype(jnp.bfloat16))
            acc = acc * lax.rsqrt(jnp.mean(acc * acc, -1, keepdims=True) + 1e-06)
            out_ref[s, at_span, cols] = jnp.where(valid, acc, 0.0).astype(jnp.bfloat16)

    def finish(s):
        total[...] = jnp.zeros_like(total)

        @pl.loop(0, span_count)
        def _(span):
            near_span(s, span)

        for bit in range(seq_bits):
            outbox[s, bit] = total[...].astype(jnp.bfloat16)
            exchange(s, bit).start()
            exchange(s, bit).wait_recv()
            if bit < seq_bits - 1:
                total[...] = total[...] + inbox[s, bit].astype(jnp.float32)

        @pl.loop(0, span_count)
        def _(span):
            far_span(s, span)

    @pl.loop(0, batch)
    def _(s):
        own_copy(s).wait()
        project(s, me)

    @pl.loop(0, (groups - 1) * batch)
    def _(event):
        d = event // batch + 1
        s = event % batch
        for side in range(2):
            owner = me - d if side == 0 else me + d
            present = owner >= 0 if side == 0 else owner < groups

            @pl.when(present)
            def _():
                pass_on(side, s, owner).wait_recv()

                @pl.when(has_next(side))
                def _():
                    pass_on(side, s, owner).start()

        @pl.loop(0, 2)
        def _(way):
            owner = me - d + 2 * d * way

            @pl.when((owner >= 0) & (owner < groups))
            def _():
                project(s, owner)

        @pl.when(d == groups - 1)
        def _():
            finish(s)

    for s in range(batch):
        for side in range(2):
            @pl.when(has_next(side))
            def _():
                send_own(side, s).wait_send()

                for d in range(1, groups - 1):
                    owner = me - d if side == 0 else me + d

                    @pl.when(owner >= 0 if side == 0 else owner < groups)
                    def _():
                        pass_on(side, s, owner).wait_send()

        for bit in range(seq_bits):
            exchange(s, bit).wait_send()


def on_device(tokens, norm_gain, projection, level_table, level_index, lengths):
    batch, row_count, model_width = tokens.shape
    table_count, heads, level_total = level_table.shape
    width = projection.shape[1]
    head_size = width // (3 * heads)
    groups = lax.axis_size("head")
    block_len = row_count * groups
    span_count = block_len // SPAN
    seq_bits = lax.axis_size("seq").bit_length() - 1
    table = jnp.pad(level_table, ((0, 0), (0, 0), (0, STRIDE - level_total)))
    table = table.reshape(table_count, heads * STRIDE)
    out_width = heads * head_size
    vmem = pl.BlockSpec(memory_space=pltpu.VMEM)
    hbm = pl.BlockSpec(memory_space=pl.ANY)
    states = (batch, seq_bits, heads, head_size, head_size)
    return pl.pallas_call(
        functools.partial(kernel, (heads, head_size, groups, seq_bits, span_count)),
        in_specs=[hbm, vmem, hbm, vmem, vmem, pl.BlockSpec(memory_space=pltpu.SMEM)],
        out_specs=vmem,
        out_shape=jax.ShapeDtypeStruct((batch, block_len, out_width), jnp.bfloat16),
        scratch_shapes=[
            pltpu.VMEM((batch, groups, row_count, model_width), jnp.bfloat16),
            pltpu.VMEM((model_width, width), jnp.bfloat16),
            pltpu.VMEM((row_count, model_width), jnp.bfloat16),
            pltpu.VMEM((batch, block_len, width), jnp.bfloat16),
            pltpu.VMEM((block_len, out_width), jnp.float32),
            pltpu.VMEM((block_len, heads * STRIDE), jnp.float32),
            pltpu.VMEM((heads, head_size, head_size), jnp.float32),
            pltpu.VMEM(states, jnp.bfloat16),
            pltpu.VMEM(states, jnp.bfloat16),
            pltpu.SemaphoreType.DMA((batch,)),
            pltpu.SemaphoreType.DMA,
            pltpu.SemaphoreType.DMA((2, batch, groups)),
            pltpu.SemaphoreType.DMA((batch, groups)),
            pltpu.SemaphoreType.DMA((batch, seq_bits)),
            pltpu.SemaphoreType.DMA((batch, seq_bits)),
        ],
        compiler_params=pltpu.CompilerParams(
            vmem_limit_bytes=VMEM_LIMIT, collective_id=0, has_side_effects=True
        ),
        name="attend",
    )(tokens, norm_gain[None], projection, table, level_index[..., None], lengths)


def solution(mesh):
    in_specs = (
        P(None, ("seq", "head"), None),
        P(),
        P(None, "head"),
        P(None, "head", None),
        P(None, "seq"),
        P(),
    )
    out_specs = P(None, "seq", "head")
    return jax.shard_map(
        on_device, mesh=mesh, in_specs=in_specs, out_specs=out_specs, check_vma=False
    )
```

```python
import functools

import jax
import jax.numpy as jnp
from jax import lax
from jax.experimental import pallas as pl
from jax.experimental.pallas import tpu as pltpu
from jax.sharding import PartitionSpec as P

SPAN = 512
LANE = 128
STRIDE = 32
VMEM_LIMIT = 56 * 1024 * 1024
NT = (((1,), (1,)), ((), ()))
TN = (((0,), (0,)), ((), ()))
MESH = pl.DeviceIdType.MESH


def dot32(a, b):
    return jnp.dot(a, b, preferred_element_type=jnp.float32)


def kernel(
    dims,
    tokens_ref, gain_ref, proj_hbm, table_ref, index_ref, lengths_ref,
    out_ref,
    rows_buf, proj_ref, normed, qkv, near, weights, states, total, outbox, inbox,
    own_sem, proj_sem, send_sem, recv_sem, tree_send, tree_recv,
):
    heads, head_size, groups, seq_bits, span_count = dims
    batch, row_count, model_width = tokens_ref.shape
    block_len = row_count * groups
    width = proj_ref.shape[1]
    lchunk = SPAN.bit_length() - 1
    local_bits = span_count.bit_length() - 1
    shards = SPAN // row_count
    first_level = lchunk + local_bits + 1
    me = lax.axis_index("head")
    own = lax.axis_index("seq")

    def flipped(bit):
        return own + (1 << bit) - 2 * (own & (1 << bit))

    proj_copy = pltpu.make_async_copy(proj_hbm, proj_ref, proj_sem)
    barrier = pltpu.get_barrier_semaphore()

    @pl.when(me > 0)
    def _():
        pl.semaphore_signal(barrier, inc=1, device_id={"head": me - 1}, device_id_type=MESH)

    @pl.when(me < groups - 1)
    def _():
        pl.semaphore_signal(barrier, inc=1, device_id={"head": me + 1}, device_id_type=MESH)

    for bit in range(seq_bits):
        pl.semaphore_signal(barrier, inc=1, device_id={"seq": flipped(bit)}, device_id_type=MESH)

    def own_copy(s):
        return pltpu.make_async_copy(tokens_ref.at[s], rows_buf.at[s, me], own_sem.at[s])

    for s in range(batch):
        own_copy(s).start()
    proj_copy.start()
    ends = (me == 0).astype(jnp.int32) + (me == groups - 1).astype(jnp.int32)
    pl.semaphore_wait(barrier, seq_bits + 2 - ends)

    def send_own(side, s):
        return pltpu.make_async_remote_copy(
            src_ref=tokens_ref.at[s], dst_ref=rows_buf.at[s, me],
            send_sem=send_sem.at[side, s, me], recv_sem=recv_sem.at[s, me],
            device_id={"head": me + 1 - 2 * side}, device_id_type=MESH,
        )

    def pass_on(side, s, owner):
        return pltpu.make_async_remote_copy(
            src_ref=rows_buf.at[s, owner], dst_ref=rows_buf.at[s, owner],
            send_sem=send_sem.at[side, s, owner], recv_sem=recv_sem.at[s, owner],
            device_id={"head": me + 1 - 2 * side}, device_id_type=MESH,
        )

    def has_next(side):
        return me < groups - 1 if side == 0 else me > 0

    for s in range(batch):
        for side in range(2):
            @pl.when(has_next(side))
            def _():
                send_own(side, s).start()

    def project(s, owner):
        piece = 128
        for start in range(0, row_count, piece):
            x = rows_buf[s, owner, start : start + piece].astype(jnp.float32)
            scale = lax.rsqrt(jnp.mean(x * x, -1, keepdims=True) + 1e-06)
            normed[start : start + piece] = (x * scale * gain_ref[...]).astype(jnp.bfloat16)
        step = 2 * 3 * head_size if width % (6 * head_size) == 0 else 3 * head_size
        at = pl.ds(pl.multiple_of(owner * row_count, row_count), row_count)
        for col in range(0, width, step):
            qkv[s, at, col : col + step] = dot32(
                normed[...], proj_ref[:, col : col + step]
            ).astype(jnp.bfloat16)

    t = lax.broadcasted_iota(jnp.int32, (LANE, LANE), 0)
    u = lax.broadcasted_iota(jnp.int32, (LANE, LANE), 1)
    apart = t ^ u
    level = jnp.zeros((LANE, LANE), jnp.int32)
    for shift in range(LANE.bit_length() - 1):
        level = level + (apart >= 1 << shift).astype(jnp.int32)
    level = jnp.where(u <= t, level, STRIDE - 1)

    for s in range(batch):
        for start in range(0, block_len, SPAN):
            tables = lax.broadcasted_iota(jnp.int32, (table_ref.shape[0], SPAN), 0)
            onehot = (index_ref[s : s + 1, start : start + SPAN] == tables).astype(jnp.float32)
            weights[s, start : start + SPAN, :] = lax.dot_general(
                onehot, table_ref[...], TN, precision=lax.Precision.HIGHEST,
                preferred_element_type=jnp.float32,
            )

    proj_copy.wait()

    def span_states(s, span):
        at_span = pl.ds(pl.multiple_of(span * SPAN, SPAN), SPAN)
        for h in range(heads):
            base = h * 3 * head_size
            k = qkv[s, at_span, base + head_size : base + 2 * head_size]
            v = qkv[s, at_span, base + 2 * head_size : base + 3 * head_size]
            states[s, span, h] = lax.dot_general(k, v, TN, preferred_element_type=jnp.float32)

    def near_head(s, span, h):
        base_row = span * SPAN
        at_span = pl.ds(pl.multiple_of(base_row, SPAN), SPAN)
        base = h * 3 * head_size
        q = qkv[s, at_span, base : base + head_size]
        k = qkv[s, at_span, base + head_size : base + 2 * head_size]
        v = qkv[s, at_span, base + 2 * head_size : base + 3 * head_size]
        out_cols = slice(h * head_size, (h + 1) * head_size)
        for start in range(0, SPAN, LANE):
            rows = slice(start, start + LANE)
            at_rows = pl.ds(pl.multiple_of(base_row + start, LANE), LANE)
            w_rows = weights[s, at_rows, :]
            grid = jnp.take_along_axis(w_rows, level + h * STRIDE, axis=1)
            scores = lax.dot_general(q[rows], k[rows], NT, preferred_element_type=jnp.float32)
            acc = dot32((scores * grid).astype(jnp.bfloat16), v[rows])
            size = LANE
            while size < SPAN:
                if start & size:
                    low = start & ~(2 * size - 1)
                    at = h * STRIDE + size.bit_length()
                    scores = lax.dot_general(
                        q[rows], k[low : low + size], NT, preferred_element_type=jnp.float32
                    )
                    scores = (scores * w_rows[:, at : at + 1]).astype(jnp.bfloat16)
                    acc = acc + dot32(scores, v[low : low + size])
                size *= 2
            near[s, at_rows, out_cols] = acc

    def exchange(s, bit):
        return pltpu.make_async_remote_copy(
            src_ref=outbox.at[s, bit], dst_ref=inbox.at[s, bit],
            send_sem=tree_send.at[s, bit], recv_sem=tree_recv.at[s, bit],
            device_id={"seq": flipped(bit)}, device_id_type=MESH,
        )

    def far_span(s, span):
        base_row = span * SPAN
        at_span = pl.ds(pl.multiple_of(base_row, SPAN), SPAN)
        first = own * block_len + base_row
        valid = first + lax.broadcasted_iota(jnp.int32, (SPAN, 1), 0) < lengths_ref[s]
        w_rows = weights[s, at_span, :]
        for h in range(heads):
            cols = slice(h * head_size, (h + 1) * head_size)
            base = h * 3 * head_size
            q = qkv[s, at_span, base : base + head_size]
            acc = near[s, at_span, cols]
            for j in range(span_count - 1):
                earlier = jnp.where(span > j, states[s, j, h], 0.0).astype(jnp.bfloat16)
                at = h * STRIDE + lchunk + 1
                acc = acc + w_rows[:, at : at + 1] * dot32(q, earlier)
            for j in range(seq_bits):
                upper = ((own >> j) & 1) == 1
                bucket = jnp.where(upper, inbox[s, j, h].astype(jnp.float32), 0.0)
                at = h * STRIDE + first_level + j
                acc = acc + w_rows[:, at : at + 1] * dot32(q, bucket.astype(jnp.bfloat16))
            acc = acc * lax.rsqrt(jnp.mean(acc * acc, -1, keepdims=True) + 1e-06)
            out_ref[s, at_span, cols] = jnp.where(valid, acc, 0.0).astype(jnp.bfloat16)

    def last_shard(span):
        low = span * shards
        high = low + shards - 1
        return jnp.maximum(jnp.maximum(me - low, low - me), jnp.maximum(me - high, high - me))

    chunk = -(-heads // seq_bits)

    def finish(s):
        summed = states[s, 0]
        for span in range(1, span_count):
            summed = summed + states[s, span]
        total[...] = summed
        for bit in range(seq_bits):
            outbox[s, bit] = total[...].astype(jnp.bfloat16)
            exchange(s, bit).start()
            for h in range(bit * chunk, min(heads, (bit + 1) * chunk)):
                @pl.loop(0, span_count)
                def _(span):
                    @pl.when(last_shard(span) == groups - 1)
                    def _():
                        near_head(s, span, h)
            exchange(s, bit).wait_recv()
            if bit < seq_bits - 1:
                total[...] = total[...] + inbox[s, bit].astype(jnp.float32)

        @pl.loop(0, span_count)
        def _(span):
            far_span(s, span)

    @pl.loop(0, batch)
    def _(s):
        own_copy(s).wait()
        project(s, me)

    @pl.loop(0, (groups - 1) * batch)
    def _(event):
        d = event // batch + 1
        s = event % batch
        for side in range(2):
            owner = me - d if side == 0 else me + d
            present = owner >= 0 if side == 0 else owner < groups

            @pl.when(present)
            def _():
                pass_on(side, s, owner).wait_recv()

                @pl.when(has_next(side))
                def _():
                    pass_on(side, s, owner).start()

        @pl.loop(0, 2)
        def _(way):
            owner = me - d + 2 * d * way

            @pl.when((owner >= 0) & (owner < groups))
            def _():
                project(s, owner)

        @pl.loop(0, span_count)
        def _(span):
            @pl.when(last_shard(span) == d)
            def _():
                span_states(s, span)

                @pl.when(d < groups - 1)
                def _():
                    for h in range(heads):
                        near_head(s, span, h)

        @pl.when(d == groups - 1)
        def _():
            finish(s)

    for s in range(batch):
        for side in range(2):
            @pl.when(has_next(side))
            def _():
                send_own(side, s).wait_send()

                for d in range(1, groups - 1):
                    owner = me - d if side == 0 else me + d

                    @pl.when(owner >= 0 if side == 0 else owner < groups)
                    def _():
                        pass_on(side, s, owner).wait_send()

        for bit in range(seq_bits):
            exchange(s, bit).wait_send()


def on_device(tokens, norm_gain, projection, level_table, level_index, lengths):
    batch, row_count, model_width = tokens.shape
    table_count, heads, level_total = level_table.shape
    width = projection.shape[1]
    head_size = width // (3 * heads)
    groups = lax.axis_size("head")
    block_len = row_count * groups
    span_count = block_len // SPAN
    seq_bits = lax.axis_size("seq").bit_length() - 1
    table = jnp.pad(level_table, ((0, 0), (0, 0), (0, STRIDE - level_total)))
    table = table.reshape(table_count, heads * STRIDE)
    out_width = heads * head_size
    vmem = pl.BlockSpec(memory_space=pltpu.VMEM)
    hbm = pl.BlockSpec(memory_space=pl.ANY)
    states = (batch, seq_bits, heads, head_size, head_size)
    return pl.pallas_call(
        functools.partial(kernel, (heads, head_size, groups, seq_bits, span_count)),
        in_specs=[hbm, vmem, hbm, vmem, vmem, pl.BlockSpec(memory_space=pltpu.SMEM)],
        out_specs=vmem,
        out_shape=jax.ShapeDtypeStruct((batch, block_len, out_width), jnp.bfloat16),
        scratch_shapes=[
            pltpu.VMEM((batch, groups, row_count, model_width), jnp.bfloat16),
            pltpu.VMEM((model_width, width), jnp.bfloat16),
            pltpu.VMEM((row_count, model_width), jnp.bfloat16),
            pltpu.VMEM((batch, block_len, width), jnp.bfloat16),
            pltpu.VMEM((batch, block_len, out_width), jnp.float32),
            pltpu.VMEM((batch, block_len, heads * STRIDE), jnp.float32),
            pltpu.VMEM((batch, span_count, heads, head_size, head_size), jnp.float32),
            pltpu.VMEM((heads, head_size, head_size), jnp.float32),
            pltpu.VMEM(states, jnp.bfloat16),
            pltpu.VMEM(states, jnp.bfloat16),
            pltpu.SemaphoreType.DMA((batch,)),
            pltpu.SemaphoreType.DMA,
            pltpu.SemaphoreType.DMA((2, batch, groups)),
            pltpu.SemaphoreType.DMA((batch, groups)),
            pltpu.SemaphoreType.DMA((batch, seq_bits)),
            pltpu.SemaphoreType.DMA((batch, seq_bits)),
        ],
        compiler_params=pltpu.CompilerParams(
            vmem_limit_bytes=VMEM_LIMIT, collective_id=0, has_side_effects=True
        ),
        name="attend",
    )(tokens, norm_gain[None], projection, table, level_index, lengths)


def solution(mesh):
    in_specs = (
        P(None, ("seq", "head"), None),
        P(),
        P(None, "head"),
        P(None, "head", None),
        P(None, "seq"),
        P(),
    )
    out_specs = P(None, "seq", "head")
    return jax.shard_map(
        on_device, mesh=mesh, in_specs=in_specs, out_specs=out_specs, check_vma=False
    )
```

```python
import functools

import jax
import jax.numpy as jnp
from jax import lax
from jax.experimental import pallas as pl
from jax.experimental.pallas import tpu as pltpu
from jax.sharding import PartitionSpec as P

SPAN = 512
LANE = 128
STRIDE = 32
VMEM_LIMIT = 56 * 1024 * 1024
NT = (((1,), (1,)), ((), ()))
TN = (((0,), (0,)), ((), ()))
MESH = pl.DeviceIdType.MESH


def dot32(a, b):
    return jnp.dot(a, b, preferred_element_type=jnp.float32)


def kernel(
    dims,
    tokens_ref, gain_ref, proj_hbm, table_ref, index_ref, lengths_ref,
    out_ref,
    rows_buf, proj_ref, normed, qkv, near, weights, states, total, outbox, inbox,
    own_sem, proj_sem, send_sem, recv_sem, tree_send, tree_recv,
):
    heads, head_size, groups, seq_bits, span_count = dims
    batch, row_count, model_width = tokens_ref.shape
    block_len = row_count * groups
    width = proj_ref.shape[1]
    lchunk = SPAN.bit_length() - 1
    local_bits = span_count.bit_length() - 1
    shards = SPAN // row_count
    first_level = lchunk + local_bits + 1
    me = lax.axis_index("head")
    own = lax.axis_index("seq")

    def flipped(bit):
        return own + (1 << bit) - 2 * (own & (1 << bit))

    proj_copy = pltpu.make_async_copy(proj_hbm, proj_ref, proj_sem)
    barrier = pltpu.get_barrier_semaphore()

    @pl.when(me > 0)
    def _():
        pl.semaphore_signal(barrier, inc=1, device_id={"head": me - 1}, device_id_type=MESH)

    @pl.when(me < groups - 1)
    def _():
        pl.semaphore_signal(barrier, inc=1, device_id={"head": me + 1}, device_id_type=MESH)

    for bit in range(seq_bits):
        pl.semaphore_signal(barrier, inc=1, device_id={"seq": flipped(bit)}, device_id_type=MESH)

    def own_copy(s):
        return pltpu.make_async_copy(tokens_ref.at[s], rows_buf.at[s, me], own_sem.at[s])

    for s in range(batch):
        own_copy(s).start()
    proj_copy.start()
    ends = (me == 0).astype(jnp.int32) + (me == groups - 1).astype(jnp.int32)
    pl.semaphore_wait(barrier, seq_bits + 2 - ends)

    def send_own(side, s):
        return pltpu.make_async_remote_copy(
            src_ref=tokens_ref.at[s], dst_ref=rows_buf.at[s, me],
            send_sem=send_sem.at[side, s, me], recv_sem=recv_sem.at[s, me],
            device_id={"head": me + 1 - 2 * side}, device_id_type=MESH,
        )

    def pass_on(side, s, owner):
        return pltpu.make_async_remote_copy(
            src_ref=rows_buf.at[s, owner], dst_ref=rows_buf.at[s, owner],
            send_sem=send_sem.at[side, s, owner], recv_sem=recv_sem.at[s, owner],
            device_id={"head": me + 1 - 2 * side}, device_id_type=MESH,
        )

    def has_next(side):
        return me < groups - 1 if side == 0 else me > 0

    for s in range(batch):
        for side in range(2):
            @pl.when(has_next(side))
            def _():
                send_own(side, s).start()

    def project(s, owner):
        piece = 128
        for start in range(0, row_count, piece):
            x = rows_buf[s, owner, start : start + piece].astype(jnp.float32)
            scale = lax.rsqrt(jnp.mean(x * x, -1, keepdims=True) + 1e-06)
            normed[start : start + piece] = (x * scale * gain_ref[...]).astype(jnp.bfloat16)
        step = 2 * 3 * head_size if width % (6 * head_size) == 0 else 3 * head_size
        at = pl.ds(pl.multiple_of(owner * row_count, row_count), row_count)
        for col in range(0, width, step):
            qkv[s, at, col : col + step] = dot32(
                normed[...], proj_ref[:, col : col + step]
            ).astype(jnp.bfloat16)

    t = lax.broadcasted_iota(jnp.int32, (LANE, LANE), 0)
    u = lax.broadcasted_iota(jnp.int32, (LANE, LANE), 1)
    apart = t ^ u
    level = jnp.zeros((LANE, LANE), jnp.int32)
    for shift in range(LANE.bit_length() - 1):
        level = level + (apart >= 1 << shift).astype(jnp.int32)
    level = jnp.where(u <= t, level, STRIDE - 1)

    for s in range(batch):
        for start in range(0, block_len, SPAN):
            tables = lax.broadcasted_iota(jnp.int32, (table_ref.shape[0], SPAN), 0)
            onehot = (index_ref[s : s + 1, start : start + SPAN] == tables).astype(jnp.float32)
            weights[s, start : start + SPAN, :] = lax.dot_general(
                onehot, table_ref[...], TN, precision=lax.Precision.HIGHEST,
                preferred_element_type=jnp.float32,
            )

    proj_copy.wait()

    def span_states(s, span):
        at_span = pl.ds(pl.multiple_of(span * SPAN, SPAN), SPAN)
        for h in range(heads):
            base = h * 3 * head_size
            k = qkv[s, at_span, base + head_size : base + 2 * head_size]
            v = qkv[s, at_span, base + 2 * head_size : base + 3 * head_size]
            states[s, span, h] = lax.dot_general(k, v, TN, preferred_element_type=jnp.float32)

    def near_head(s, span, h):
        base_row = span * SPAN
        at_span = pl.ds(pl.multiple_of(base_row, SPAN), SPAN)
        base = h * 3 * head_size
        q = qkv[s, at_span, base : base + head_size]
        k = qkv[s, at_span, base + head_size : base + 2 * head_size]
        v = qkv[s, at_span, base + 2 * head_size : base + 3 * head_size]
        out_cols = slice(h * head_size, (h + 1) * head_size)
        for start in range(0, SPAN, LANE):
            rows = slice(start, start + LANE)
            at_rows = pl.ds(pl.multiple_of(base_row + start, LANE), LANE)
            w_rows = weights[s, at_rows, :]
            grid = jnp.take_along_axis(w_rows, level + h * STRIDE, axis=1)
            scores = lax.dot_general(q[rows], k[rows], NT, preferred_element_type=jnp.float32)
            acc = dot32((scores * grid).astype(jnp.bfloat16), v[rows])
            size = LANE
            while size < SPAN:
                if start & size:
                    low = start & ~(2 * size - 1)
                    at = h * STRIDE + size.bit_length()
                    scores = lax.dot_general(
                        q[rows], k[low : low + size], NT, preferred_element_type=jnp.float32
                    )
                    scores = (scores * w_rows[:, at : at + 1]).astype(jnp.bfloat16)
                    acc = acc + dot32(scores, v[low : low + size])
                size *= 2
            near[s, at_rows, out_cols] = acc

    def exchange(s, bit):
        return pltpu.make_async_remote_copy(
            src_ref=outbox.at[s, bit], dst_ref=inbox.at[s, bit],
            send_sem=tree_send.at[s, bit], recv_sem=tree_recv.at[s, bit],
            device_id={"seq": flipped(bit)}, device_id_type=MESH,
        )

    def bucket_part(s, h, j, q, w_rows):
        upper = ((own >> j) & 1) == 1
        bucket = jnp.where(upper, inbox[s, j, h].astype(jnp.float32), 0.0)
        at = h * STRIDE + first_level + j
        return w_rows[:, at : at + 1] * dot32(q, bucket.astype(jnp.bfloat16))

    def far_early(s, span):
        at_span = pl.ds(pl.multiple_of(span * SPAN, SPAN), SPAN)
        w_rows = weights[s, at_span, :]
        for h in range(heads):
            cols = slice(h * head_size, (h + 1) * head_size)
            base = h * 3 * head_size
            q = qkv[s, at_span, base : base + head_size]
            acc = near[s, at_span, cols]
            for j in range(span_count - 1):
                earlier = jnp.where(span > j, states[s, j, h], 0.0).astype(jnp.bfloat16)
                at = h * STRIDE + lchunk + 1
                acc = acc + w_rows[:, at : at + 1] * dot32(q, earlier)
            for j in range(seq_bits - 1):
                acc = acc + bucket_part(s, h, j, q, w_rows)
            near[s, at_span, cols] = acc

    def far_last(s, span):
        base_row = span * SPAN
        at_span = pl.ds(pl.multiple_of(base_row, SPAN), SPAN)
        first = own * block_len + base_row
        valid = first + lax.broadcasted_iota(jnp.int32, (SPAN, 1), 0) < lengths_ref[s]
        w_rows = weights[s, at_span, :]
        for h in range(heads):
            cols = slice(h * head_size, (h + 1) * head_size)
            base = h * 3 * head_size
            q = qkv[s, at_span, base : base + head_size]
            acc = near[s, at_span, cols] + bucket_part(s, h, seq_bits - 1, q, w_rows)
            acc = acc * lax.rsqrt(jnp.mean(acc * acc, -1, keepdims=True) + 1e-06)
            out_ref[s, at_span, cols] = jnp.where(valid, acc, 0.0).astype(jnp.bfloat16)

    def last_shard(span):
        low = span * shards
        high = low + shards - 1
        return jnp.maximum(jnp.maximum(me - low, low - me), jnp.maximum(me - high, high - me))

    chunk = -(-heads // seq_bits)

    def finish(s):
        summed = states[s, 0]
        for span in range(1, span_count):
            summed = summed + states[s, span]
        total[...] = summed
        for bit in range(seq_bits):
            outbox[s, bit] = total[...].astype(jnp.bfloat16)
            exchange(s, bit).start()
            for h in range(bit * chunk, min(heads, (bit + 1) * chunk)):
                @pl.loop(0, span_count)
                def _(span):
                    @pl.when(last_shard(span) == groups - 1)
                    def _():
                        near_head(s, span, h)
            if bit == seq_bits - 1:
                @pl.loop(0, span_count)
                def _(span):
                    far_early(s, span)

            exchange(s, bit).wait_recv()
            if bit < seq_bits - 1:
                total[...] = total[...] + inbox[s, bit].astype(jnp.float32)

        @pl.loop(0, span_count)
        def _(span):
            far_last(s, span)

    @pl.loop(0, batch)
    def _(s):
        own_copy(s).wait()
        project(s, me)

    @pl.loop(0, (groups - 1) * batch)
    def _(event):
        d = event // batch + 1
        s = event % batch
        for side in range(2):
            owner = me - d if side == 0 else me + d
            present = owner >= 0 if side == 0 else owner < groups

            @pl.when(present)
            def _():
                pass_on(side, s, owner).wait_recv()

                @pl.when(has_next(side))
                def _():
                    pass_on(side, s, owner).start()

        @pl.loop(0, 2)
        def _(way):
            owner = me - d + 2 * d * way

            @pl.when((owner >= 0) & (owner < groups))
            def _():
                project(s, owner)

        @pl.loop(0, span_count)
        def _(span):
            @pl.when(last_shard(span) == d)
            def _():
                span_states(s, span)

                @pl.when(d < groups - 1)
                def _():
                    for h in range(heads):
                        near_head(s, span, h)

        @pl.when(d == groups - 1)
        def _():
            finish(s)

    for s in range(batch):
        for side in range(2):
            @pl.when(has_next(side))
            def _():
                send_own(side, s).wait_send()

                for d in range(1, groups - 1):
                    owner = me - d if side == 0 else me + d

                    @pl.when(owner >= 0 if side == 0 else owner < groups)
                    def _():
                        pass_on(side, s, owner).wait_send()

        for bit in range(seq_bits):
            exchange(s, bit).wait_send()


def on_device(tokens, norm_gain, projection, level_table, level_index, lengths):
    batch, row_count, model_width = tokens.shape
    table_count, heads, level_total = level_table.shape
    width = projection.shape[1]
    head_size = width // (3 * heads)
    groups = lax.axis_size("head")
    block_len = row_count * groups
    span_count = block_len // SPAN
    seq_bits = lax.axis_size("seq").bit_length() - 1
    table = jnp.pad(level_table, ((0, 0), (0, 0), (0, STRIDE - level_total)))
    table = table.reshape(table_count, heads * STRIDE)
    out_width = heads * head_size
    vmem = pl.BlockSpec(memory_space=pltpu.VMEM)
    hbm = pl.BlockSpec(memory_space=pl.ANY)
    states = (batch, seq_bits, heads, head_size, head_size)
    return pl.pallas_call(
        functools.partial(kernel, (heads, head_size, groups, seq_bits, span_count)),
        in_specs=[hbm, vmem, hbm, vmem, vmem, pl.BlockSpec(memory_space=pltpu.SMEM)],
        out_specs=vmem,
        out_shape=jax.ShapeDtypeStruct((batch, block_len, out_width), jnp.bfloat16),
        scratch_shapes=[
            pltpu.VMEM((batch, groups, row_count, model_width), jnp.bfloat16),
            pltpu.VMEM((model_width, width), jnp.bfloat16),
            pltpu.VMEM((row_count, model_width), jnp.bfloat16),
            pltpu.VMEM((batch, block_len, width), jnp.bfloat16),
            pltpu.VMEM((batch, block_len, out_width), jnp.float32),
            pltpu.VMEM((batch, block_len, heads * STRIDE), jnp.float32),
            pltpu.VMEM((batch, span_count, heads, head_size, head_size), jnp.float32),
            pltpu.VMEM((heads, head_size, head_size), jnp.float32),
            pltpu.VMEM(states, jnp.bfloat16),
            pltpu.VMEM(states, jnp.bfloat16),
            pltpu.SemaphoreType.DMA((batch,)),
            pltpu.SemaphoreType.DMA,
            pltpu.SemaphoreType.DMA((2, batch, groups)),
            pltpu.SemaphoreType.DMA((batch, groups)),
            pltpu.SemaphoreType.DMA((batch, seq_bits)),
            pltpu.SemaphoreType.DMA((batch, seq_bits)),
        ],
        compiler_params=pltpu.CompilerParams(
            vmem_limit_bytes=VMEM_LIMIT, collective_id=0, has_side_effects=True
        ),
        name="attend",
    )(tokens, norm_gain[None], projection, table, level_index, lengths)


def solution(mesh):
    in_specs = (
        P(None, ("seq", "head"), None),
        P(),
        P(None, "head"),
        P(None, "head", None),
        P(None, "seq"),
        P(),
    )
    out_specs = P(None, "seq", "head")
    return jax.shard_map(
        on_device, mesh=mesh, in_specs=in_specs, out_specs=out_specs, check_vma=False
    )
```
